32 devices in a mesh: curve: 16 (over z, x, core), group: 2 (over y).
Axes of the slice: x: 2, y: 2, z: 4, core: 2. Of those that a mesh axis runs over, the one named last changes fastest.
Arguments:
- field: float32 [3, 256, 64, 128], P(None, 'curve', 'group'), may hold values from -6 to 6
- source: float32 [3, 256, 64, 128], P(None, 'curve', 'group'), may hold values from -16 to 16
- mass: float32 [256, 64, 128], P('curve', 'group'), may hold values from 0.5 to 8
- interp: float32 [4, 128, 128], replicated, may hold values from -0.5 to 1.5
- parent_list: int32 [16, 2, 2, 16], P('curve', 'group'), may hold values from 0 to 511
- child_list: int32 [16, 2, 2, 16], P('curve', 'group'), may hold values from 0 to 511
- child_kind: int32 [16, 2, 2, 16], P('curve', 'group'), may hold values from 0 to 3
- counts: int32 [16, 2, 2], P('curve', 'group'), may hold values from 0 to 16, as said below
Outputs:
- cycle: float32 [3, 256, 64, 128], P(None, 'curve', 'group')
The draws below stay inside these ranges and needn't reach their ends.
Inputs may be any that keep to these rules, and one draw needn't show every extreme that they name: `parent_list`: local block index x * 32 + y on the device that owns the parent. `child_list`: local block index x * 32 + y on the device that owns the child. `counts`: in every draw, in each curve segment one destination group receives 16 live slots from every source group; every other destination group receives at most 8 live slots from each source group.
All inputs are finite; a program needn't handle non-finite values.
Results may differ from the reference program's by a relative error of at most 0.0001.
Values sent between devices are 32-bit elements; how exact they have to be, the bound alone decides.
A program may use at most 64 MiB of HBM per device.

```python
import math
import jax
import jax.numpy as jnp
from jax import lax

NODES = 128
KINDS = 4
SWEEPS = 2
XBLOCKS = 16
YBLOCKS = 32
SLOTS = 16
SEGMENTS = 16
GROUPS = 2
NX = 256
NY = 64


def draw_interp(key, part):
    noise_key = jax.random.fold_in(key, 11)
    noise = jax.random.uniform(noise_key, (KINDS, NODES, NODES), jnp.float32, -1.0, 1.0)
    identity = jnp.eye(NODES, dtype=jnp.float32)[None]
    return identity + noise * (0.9 / NODES ** 0.5)


def draw_counts(key, part):
    base = jax.random.randint(jax.random.fold_in(key, 21), (SEGMENTS, GROUPS, GROUPS), 0, SLOTS // 2 + 1)
    target = jax.random.randint(jax.random.fold_in(key, 22), (SEGMENTS,), 0, GROUPS)
    filled = jnp.arange(GROUPS)[None, None, :] == target[:, None, None]
    return jnp.where(filled, SLOTS, base).astype(jnp.int32)


def place_ends(array, own_key, low, largest):
    longest = array.shape.index(max(array.shape))
    spots = []
    for shift in (0, 1):
        where = [jax.random.randint(jax.random.fold_in(own_key, axis), (), 0, length) for axis, length in enumerate(array.shape)]
        where[longest] = (where[longest] + shift) % array.shape[longest]
        spots.append(tuple(where))
    return array.at[spots[0]].set(low).at[spots[1]].set(largest)


def level_of(key, extent, cuts, low, high):
    factor_of = 1.0
    for axis_at, parts in cuts:
        draws = jax.random.uniform(jax.random.fold_in(jax.random.fold_in(key, 6), axis_at), (parts,), jnp.float32, low / len(cuts), high / len(cuts))
        factor_of = factor_of * jnp.repeat(jnp.exp(draws), extent[axis_at] // parts).reshape((-1,) + (1,) * (len(extent) - 1 - axis_at))
    return factor_of


def bell_draw(key, extent, width, bound, split=(), kind=jnp.bfloat16):
    values = width * jax.random.normal(key, extent, jnp.float32)
    if split:
        values = values * level_of(key, extent, split, -0.22, 0.18)
    return jnp.clip(values, -bound, bound).astype(kind)


def setup_inputs(seed: int = 0) -> dict:
    splits = jax.random.split(jax.random.key(seed), 9)
    field = bell_draw(splits[0], (3, NX, NY, NODES), 1.0, 6.0, ((1, 16), (2, 2)), jnp.float32)
    source = bell_draw(splits[1], (3, NX, NY, NODES), 4.0, 16.0, ((1, 16), (2, 2)), jnp.float32)
    mass = jnp.clip(jnp.exp(math.log(8.0) - 2.7725887 * jax.random.uniform(splits[2], (NX, NY, NODES), jnp.float32) ** level_of(splits[2], (NX, NY, NODES), ((0, 16), (1, 2)), -0.2, 0.2)), 0.5, 8.0)
    interp = draw_interp(jax.random.fold_in(splits[8], 71), 0)
    parent_list = place_ends(jax.random.randint(splits[4], (SEGMENTS, GROUPS, GROUPS, SLOTS), 0, XBLOCKS * YBLOCKS), jax.random.fold_in(splits[4], 1), 0, (XBLOCKS * YBLOCKS) - 1).astype(jnp.int32)
    child_list = place_ends(jax.random.randint(splits[5], (SEGMENTS, GROUPS, GROUPS, SLOTS), 0, XBLOCKS * YBLOCKS), jax.random.fold_in(splits[5], 1), 0, (XBLOCKS * YBLOCKS) - 1).astype(jnp.int32)
    child_kind = place_ends(jax.random.randint(splits[6], (SEGMENTS, GROUPS, GROUPS, SLOTS), 0, KINDS), jax.random.fold_in(splits[6], 1), 0, KINDS - 1).astype(jnp.int32)
    counts = draw_counts(jax.random.fold_in(splits[8], 71), 0)
    return {"field": field, "source": source, "mass": mass, "interp": interp, "parent_list": parent_list, "child_list": child_list, "child_kind": child_kind, "counts": counts}


OMEGA = 2.0 / 3.0


def relax(padded, source, mass):
    centre = padded[:, 1:-1, 1:-1, :]
    beside = padded[:, 2:, 1:-1, :] + padded[:, :-2, 1:-1, :] + padded[:, 1:-1, 2:, :] + padded[:, 1:-1, :-2, :]
    z_pair = jnp.pad(centre, ((0, 0), (0, 0), (0, 0), (1, 1)))
    beside = beside + z_pair[..., 2:] + z_pair[..., :-2]
    diag_total = 6.0 + mass
    applied = diag_total * centre - beside
    return centre + OMEGA * (source - applied) / diag_total


def to_rows(whole):
    return whole.reshape(3, SEGMENTS, XBLOCKS, GROUPS, YBLOCKS, NODES).transpose(1, 3, 2, 4, 0, 5).reshape(SEGMENTS * GROUPS * XBLOCKS * YBLOCKS, 3, NODES)


def to_field(rows):
    return rows.reshape(SEGMENTS, GROUPS, XBLOCKS, YBLOCKS, 3, NODES).transpose(4, 0, 2, 1, 3, 5).reshape(3, NX, NY, NODES)


def by_kind(picked, tables, kind_faces):
    result = jnp.zeros(picked.shape, jnp.float32)
    flat = picked.reshape(-1, NODES)
    for kind_index in range(KINDS):
        product = jnp.dot(flat, tables[kind_index], precision=lax.Precision.HIGHEST, preferred_element_type=jnp.float32).reshape(picked.shape)
        weight = (kind_faces == kind_index).astype(jnp.float32)
        result = result + product * weight[..., None, None]
    return result


def reference(field, source, mass, interp, parent_list, child_list, child_kind, counts):
    block_count = XBLOCKS * YBLOCKS
    seg_ids = jnp.arange(SEGMENTS, dtype=jnp.int32)[:, None, None, None]
    src_ids = jnp.arange(GROUPS, dtype=jnp.int32)[None, :, None, None]
    dst_ids = jnp.arange(GROUPS, dtype=jnp.int32)[None, None, :, None]
    parent_rows = ((seg_ids * GROUPS + src_ids) * block_count + parent_list).astype(jnp.int32)
    child_faces = jnp.transpose(child_list, (0, 2, 1, 3))
    kind_faces = jnp.transpose(child_kind, (0, 2, 1, 3))
    child_rows = ((seg_ids * GROUPS + dst_ids) * block_count + child_faces).astype(jnp.int32)
    active = (jnp.arange(SLOTS, dtype=jnp.int32)[None, None, None, :] < counts[..., None]).astype(jnp.float32)
    rows = to_rows(field)
    picked = rows[parent_rows] * active[..., None, None]
    hanging = by_kind(picked, interp, kind_faces)
    constrained = to_field(rows.at[child_rows].add(hanging))
    state = constrained
    for sweep_index in range(SWEEPS):
        padded = jnp.pad(state, ((0, 0), (1, 1), (1, 1), (0, 0)))
        state = relax(padded, source, mass)
    correction = to_rows(state - constrained)
    restricted = by_kind(correction[child_rows], jnp.transpose(interp, (0, 2, 1)), kind_faces) * active[..., None, None]
    returned = jnp.zeros_like(rows).at[parent_rows].add(restricted)
    return state + to_field(returned)
```

```python
import functools

import jax
import jax.numpy as jnp
from jax import lax
from jax.experimental import pallas as pl
from jax.experimental.pallas import tpu as pltpu
from jax.sharding import PartitionSpec as P

OMEGA = 2.0 / 3.0
KEEP = 1.0 / 3.0
MESH = pl.DeviceIdType.MESH
NT = (((1,), (1,)), ((), ()))


def split(value):
    high = value.astype(jnp.bfloat16)
    low = (value - high.astype(jnp.float32)).astype(jnp.bfloat16)
    return high, low


def column(row, size):
    first = lax.broadcasted_iota(jnp.int32, (size, size), 0)
    second = lax.broadcasted_iota(jnp.int32, (size, size), 1)
    spread = jnp.where(first == second, jnp.broadcast_to(row.astype(jnp.float32), (size, size)), 0.0)
    return jnp.sum(spread, axis=1, keepdims=True)


def lane_row(columns, slots):
    groups = len(columns)
    width = 2 * groups * slots
    first = lax.broadcasted_iota(jnp.int32, (slots, width), 0)
    second = lax.broadcasted_iota(jnp.int32, (slots, width), 1)
    total = jnp.zeros((slots, width), jnp.float32)
    for half in range(2):
        for group, col in enumerate(columns):
            base = (half * groups + group) * slots
            total = total + jnp.where(second - base == first, jnp.broadcast_to(col, (slots, width)), 0.0)
    return jnp.sum(total, axis=0, keepdims=True).astype(jnp.int32)


def kernel(
    curve_size, groups, rows_x, rows_y, nodes, slots, kinds, comps,
    field, source, mass, interp, parent_s, child_s, counts_s, parent_v, child_v, kind_v,
    out,
    con, mid, fin, src, wts, rhs, tab, pick, arr, base_rows, now_rows, res, back,
    x_in, y_out, y_in, s_out, s_in, k_out, k_in, y_mid, ext,
    load_sem, out_sem, send_sem, recv_sem, pick_send, pick_recv, back_send, back_recv,
):
    f32 = jnp.float32
    blocks = rows_x * rows_y
    mem = comps * slots
    c = lax.axis_index("curve")
    g = lax.axis_index("group")
    has_x = (c > 0, c < curve_size - 1)
    has_y = (g > 0, g < groups - 1)
    step = (-1, 1)

    loads = [
        pltpu.make_async_copy(field, con.at[:, pl.ds(rows_y, blocks), :], load_sem.at[0]),
        pltpu.make_async_copy(mass, wts.at[pl.ds(rows_y, blocks), :], load_sem.at[1]),
        pltpu.make_async_copy(source, src.at[:, pl.ds(rows_y, blocks), :], load_sem.at[2]),
        pltpu.make_async_copy(interp, tab, load_sem.at[3]),
    ]
    for load in loads:
        load.start()

    barrier = pltpu.get_barrier_semaphore()
    for o in range(1, groups):
        pl.semaphore_signal(barrier, inc=1, device_id=(c, lax.rem(g + o, groups)), device_id_type=MESH)
    for a in range(2):
        @pl.when(has_x[a])
        def _():
            pl.semaphore_signal(barrier, inc=1, device_id=(c + step[a], g), device_id_type=MESH)
        for b in range(2):
            @pl.when(jnp.logical_and(has_x[a], has_y[b]))
            def _():
                pl.semaphore_signal(barrier, inc=1, device_id=(c + step[a], g + step[b]), device_id_type=MESH)
    one = lambda flag: jnp.where(flag, 1, 0)
    wide = one(has_x[0]) + one(has_x[1])
    tall = one(has_y[0]) + one(has_y[1])
    pl.semaphore_wait(barrier, groups - 1 + wide + wide * tall)

    def remote(src_ref, dst_ref, sent, landed, device):
        return pltpu.make_async_remote_copy(
            src_ref=src_ref, dst_ref=dst_ref, send_sem=send_sem.at[sent], recv_sem=recv_sem.at[landed],
            device_id=device, device_id_type=MESH,
        )

    def source_x(a, arriving=False):
        side = a if arriving else 1 - a
        edge = 0 if a == 0 else blocks - rows_y
        land = 0 if side == 0 else blocks + rows_y
        there = (c + step[a], g)
        return (
            remote(source.at[:, pl.ds(edge, rows_y), :], src.at[:, pl.ds(land, rows_y), :], a, side, there),
            remote(mass.at[pl.ds(edge, rows_y), :], wts.at[pl.ds(land, rows_y), :], 2 + a, 2 + side, there),
        )

    def source_y(b, arriving=False):
        side = b if arriving else 1 - b
        return remote(s_out.at[b], s_in.at[side], 4 + b, 4 + side, (c, g + step[b]))

    def halo_x(a, arriving=False):
        side = a if arriving else 1 - a
        edge = rows_y if a == 0 else blocks - rows_y
        return remote(con.at[:, pl.ds(edge, 2 * rows_y), :], x_in.at[side], 6 + a, 6 + side, (c + step[a], g))

    def halo_y(b, arriving=False):
        side = b if arriving else 1 - b
        return remote(y_out.at[b], y_in.at[side], 8 + b, 8 + side, (c, g + step[b]))

    def corner(a, b, arriving=False):
        side = 2 * a + b if arriving else 2 * (1 - a) + (1 - b)
        return remote(k_out.at[2 * a + b], k_in.at[side], 10 + 2 * a + b, 10 + side, (c + step[a], g + step[b]))

    def picks(o):
        d = lax.rem(g + o, groups)
        return pltpu.make_async_remote_copy(
            src_ref=pick.at[o], dst_ref=arr.at[g], send_sem=pick_send.at[o], recv_sem=pick_recv.at[o],
            device_id=(c, d), device_id_type=MESH,
        )

    def returns(o):
        d = lax.rem(g + o, groups)
        return pltpu.make_async_remote_copy(
            src_ref=res.at[d], dst_ref=back.at[g], send_sem=back_send.at[o], recv_sem=back_recv.at[o],
            device_id=(c, d), device_id_type=MESH,
        )

    loads[0].wait()
    slot_of = lax.broadcasted_iota(jnp.int32, (slots, nodes), 0)
    for o in list(range(1, groups)) + [0]:
        d = lax.rem(g + o, groups)
        for k in range(slots):
            p = parent_s[0, 0, d, k]
            for m in range(comps):
                pick[o, pl.ds(m * slots + k, 1), :] = con[m, pl.ds(rows_y + p, 1), :]
        live = slot_of < counts_s[0, 0, d]
        for m in range(comps):
            part = pl.ds(m * slots, slots)
            pick[o, part, :] = jnp.where(live, pick[o, part, :], 0.0)
        if o:
            picks(o).start()
    arr[g] = pick[0]

    for a in range(2):
        @pl.when(has_x[a])
        def _():
            for copy in source_x(a):
                copy.start()

    loads[1].wait()
    loads[2].wait()
    for b in range(2):
        row = 0 if b == 0 else rows_y - 1
        for m in range(comps):
            s_out[b, pl.ds(m * rows_x, rows_x), :] = src[m, pl.ds(rows_y + row, rows_x, stride=rows_y), :]
        s_out[b, pl.ds(comps * rows_x, rows_x), :] = wts[pl.ds(rows_y + row, rows_x, stride=rows_y), :]

        @pl.when(has_y[b])
        def _():
            source_y(b).start()

    span = 2 * rows_y if rows_x % 2 == 0 else rows_y
    spans = blocks // span
    for t in range(spans):
        rows = pl.ds(rows_y + t * span, span)
        w = OMEGA / (6.0 + wts[rows, :])
        ext[pl.ds(rows_y + t * span, span), :] = w
        for m in range(comps):
            rhs[m, rows, :] = w * src[m, rows, :]
    zero_plane = jnp.zeros((rows_y, nodes), f32)
    for m in range(comps):
        con[m, pl.ds(0, rows_y), :] = zero_plane
        con[m, pl.ds(blocks + rows_y, rows_y), :] = zero_plane
    loads[3].wait()
    tab_high, tab_low = split(tab[...])
    kind_now = kind_v[0, 0]
    child_now = child_v[0, 0]
    parent_now = parent_v[0, 0]
    kind_of = []
    for s in range(groups):
        kind_col = jnp.broadcast_to(column(kind_now[s:s + 1, :], slots), (slots, nodes))
        kind_of += [kind_col] * comps
    kind_of = jnp.concatenate(kind_of, axis=0)
    child_row = lane_row([column(child_now[s:s + 1, :], slots) for s in range(groups)], slots)
    live_cols = []
    for s in range(groups):
        col = column(parent_now[s:s + 1, :], slots)
        ahead = lax.broadcasted_iota(jnp.int32, (slots, 1), 0) < counts_s[0, 0, s]
        live_cols.append(jnp.where(ahead, col, -1.0))
    parent_row = lane_row(live_cols, slots)

    def table_of(values):
        pieces = []
        for s in range(groups):
            pieces.append(jnp.concatenate(
                [values[(s * comps + m) * slots:(s * comps + m + 1) * slots, :] for m in range(comps)], axis=1))
        high, low = split(jnp.concatenate(pieces, axis=0))
        return jnp.concatenate([high, low], axis=0)

    piece = 4 * rows_y if rows_x % 4 == 0 else rows_y
    pieces = blocks // piece

    def spread(index_row, table, t):
        place = lax.broadcasted_iota(jnp.int32, (piece, 2 * groups * slots), 0) + t * piece
        hot = jnp.where(place == index_row, 1.0, 0.0).astype(jnp.bfloat16)
        return jnp.dot(hot, table, preferred_element_type=f32)

    for o in range(1, groups):
        picks(o).wait_recv()
    flat = arr[...].reshape(groups * mem, nodes)
    wide_rows = jnp.concatenate([jnp.where(kind_of == float(k), flat, 0.0) for k in range(kinds)], axis=1)
    high, low = split(wide_rows)
    hang = (
        jnp.dot(high, tab_high, preferred_element_type=f32)
        + jnp.dot(high, tab_low, preferred_element_type=f32)
        + jnp.dot(low, tab_high, preferred_element_type=f32)
    )
    table = table_of(hang)
    order = [0, pieces - 1] + list(range(1, pieces - 1))
    for at, t in enumerate(order):
        added = spread(child_row, table, t)
        for m in range(comps):
            rows = pl.ds(rows_y + t * piece, piece)
            con[m, rows, :] = con[m, rows, :] + added[:, m * nodes:(m + 1) * nodes]
        if at == 1:
            for a in range(2):
                @pl.when(has_x[a])
                def _():
                    halo_x(a).start()
            for a in range(2):
                for b in range(2):
                    x = 0 if a == 0 else rows_x - 1
                    y = 0 if b == 0 else rows_y - 1
                    for m in range(comps):
                        k_out[2 * a + b, pl.ds(m, 1), :] = con[m, pl.ds(rows_y + x * rows_y + y, 1), :]

                    @pl.when(jnp.logical_and(has_x[a], has_y[b]))
                    def _():
                        corner(a, b).start()
    for b in range(2):
        for j in range(2):
            row = j if b == 0 else rows_y - 1 - j
            for m in range(comps):
                y_out[b, pl.ds((j * comps + m) * rows_x, rows_x), :] = con[m, pl.ds(rows_y + row, rows_x, stride=rows_y), :]

        @pl.when(has_y[b])
        def _():
            halo_y(b).start()

    lane = lax.broadcasted_iota(jnp.int32, (1, nodes), 1)

    def along_z(v):
        up = jnp.where(lane == 0, 0.0, pltpu.roll(v, 1, 1))
        down = jnp.where(lane == nodes - 1, 0.0, pltpu.roll(v, nodes - 1, 1))
        return up + down

    sub = lax.broadcasted_iota(jnp.int32, (span, nodes), 0)
    is_first = sub == 0
    is_last = sub == rows_y - 1
    for t in range(1, span // rows_y):
        is_first = jnp.logical_or(is_first, sub == t * rows_y)
        is_last = jnp.logical_or(is_last, sub == (t + 1) * rows_y - 1)

    def core(state, m, t):
        at = rows_y + t * span
        centre = state[m, pl.ds(at, span), :]
        beside = state[m, pl.ds(at - rows_y, span), :] + state[m, pl.ds(at + rows_y, span), :]
        beside = beside + jnp.where(is_first, 0.0, state[m, pl.ds(at - 1, span), :])
        beside = beside + jnp.where(is_last, 0.0, state[m, pl.ds(at + 1, span), :])
        beside = beside + along_z(centre)
        return KEEP * centre + ext[pl.ds(at, span), :] * beside + rhs[m, pl.ds(at, span), :]

    for t in range(spans):
        for m in range(comps):
            mid[m, pl.ds(rows_y + t * span, span), :] = core(con, m, t)

    for s in range(groups):
        for k in range(slots):
            q = child_s[0, 0, s, k]
            for m in range(comps):
                base_rows[pl.ds((s * comps + m) * slots + k, 1), :] = con[m, pl.ds(rows_y + q, 1), :]

    for a in range(2):
        for b in range(2):
            both = jnp.logical_and(has_x[a], has_y[b])

            @pl.when(both)
            def _():
                corner(a, b, True).wait_recv()

            @pl.when(jnp.logical_not(both))
            def _():
                k_in[2 * a + b] = jnp.zeros((8, nodes), f32)
    top = lax.broadcasted_iota(jnp.int32, (rows_y, nodes), 0)
    for a in range(2):
        inside = rows_y if a == 0 else blocks
        plane = 0 if a == 0 else blocks + rows_y
        near = rows_y if a == 0 else 0
        far = 0 if a == 0 else rows_y

        @pl.when(has_x[a])
        def _():
            for copy in source_x(a, True):
                copy.wait_recv()
            halo_x(a, True).wait_recv()
            w_in = ext[pl.ds(inside, rows_y), :]
            w = OMEGA / (6.0 + wts[pl.ds(plane, rows_y), :])
            for m in range(comps):
                own = x_in[a, m, pl.ds(near, rows_y), :]
                mid[m, pl.ds(inside, rows_y), :] = mid[m, pl.ds(inside, rows_y), :] + w_in * own
                beside = x_in[a, m, pl.ds(far, rows_y), :] + con[m, pl.ds(inside, rows_y), :]
                low_end = jnp.broadcast_to(k_in[2 * a, pl.ds(m, 1), :], (rows_y, nodes))
                high_end = jnp.broadcast_to(k_in[2 * a + 1, pl.ds(m, 1), :], (rows_y, nodes))
                beside = beside + jnp.where(top == 0, low_end, pltpu.roll(own, 1, 0))
                beside = beside + jnp.where(top == rows_y - 1, high_end, pltpu.roll(own, rows_y - 1, 0))
                beside = beside + along_z(own) + src[m, pl.ds(plane, rows_y), :]
                mid[m, pl.ds(plane, rows_y), :] = KEEP * own + w * beside

        @pl.when(jnp.logical_not(has_x[a]))
        def _():
            for m in range(comps):
                mid[m, pl.ds(plane, rows_y), :] = zero_plane

    left = lax.broadcasted_iota(jnp.int32, (rows_x, nodes), 0)
    for b in range(2):
        row = 0 if b == 0 else rows_y - 1
        edge = pl.ds(rows_y + row, rows_x, stride=rows_y)

        @pl.when(has_y[b])
        def _():
            source_y(b, True).wait_recv()
            halo_y(b, True).wait_recv()
            w_in = ext[edge, :]
            w = OMEGA / (6.0 + s_in[b, pl.ds(comps * rows_x, rows_x), :])
            for m in range(comps):
                own = y_in[b, pl.ds(m * rows_x, rows_x), :]
                mid[m, edge, :] = mid[m, edge, :] + w_in * own
                beside = y_in[b, pl.ds((comps + m) * rows_x, rows_x), :] + con[m, edge, :]
                low_end = jnp.broadcast_to(k_in[b, pl.ds(m, 1), :], (rows_x, nodes))
                high_end = jnp.broadcast_to(k_in[2 + b, pl.ds(m, 1), :], (rows_x, nodes))
                beside = beside + jnp.where(left == 0, low_end, pltpu.roll(own, 1, 0))
                beside = beside + jnp.where(left == rows_x - 1, high_end, pltpu.roll(own, rows_x - 1, 0))
                beside = beside + along_z(own) + s_in[b, pl.ds(m * rows_x, rows_x), :]
                y_mid[b, pl.ds(m * rows_x, rows_x), :] = KEEP * own + w * beside

    for t in range(spans):
        for m in range(comps):
            fin[m, pl.ds(t * span, span), :] = core(mid, m, t)
    for b in range(2):
        row = 0 if b == 0 else rows_y - 1

        @pl.when(has_y[b])
        def _():
            w_in = ext[pl.ds(rows_y + row, rows_x, stride=rows_y), :]
            edge = pl.ds(row, rows_x, stride=rows_y)
            for m in range(comps):
                fin[m, edge, :] = fin[m, edge, :] + w_in * y_mid[b, pl.ds(m * rows_x, rows_x), :]

    for s in range(groups):
        for k in range(slots):
            q = child_s[0, 0, s, k]
            for m in range(comps):
                now_rows[pl.ds((s * comps + m) * slots + k, 1), :] = fin[m, pl.ds(q, 1), :]
    high, low = split(now_rows[...] - base_rows[...])
    product = (
        lax.dot_general(high, tab_high, NT, preferred_element_type=f32)
        + lax.dot_general(high, tab_low, NT, preferred_element_type=f32)
        + lax.dot_general(low, tab_high, NT, preferred_element_type=f32)
    )
    chosen = jnp.zeros((groups * mem, nodes), f32)
    for k in range(kinds):
        chosen = chosen + jnp.where(kind_of == float(k), product[:, k * nodes:(k + 1) * nodes], 0.0)
    res[...] = chosen.reshape(groups, mem, nodes)
    for o in range(1, groups):
        returns(o).start()
    back[g] = res[g]
    for o in range(1, groups):
        returns(o).wait_recv()
    table = table_of(back[...].reshape(groups * mem, nodes))
    stores = []
    for t in range(pieces):
        added = spread(parent_row, table, t)
        rows = pl.ds(t * piece, piece)
        for m in range(comps):
            fin[m, rows, :] = fin[m, rows, :] + added[:, m * nodes:(m + 1) * nodes]
        store = pltpu.make_async_copy(fin.at[:, rows, :], out.at[:, rows, :], out_sem.at[t])
        store.start()
        stores.append(store)

    for o in range(1, groups):
        picks(o).wait_send()
        returns(o).wait_send()
    for a in range(2):
        @pl.when(has_x[a])
        def _():
            for copy in source_x(a):
                copy.wait_send()
            halo_x(a).wait_send()

        @pl.when(has_y[a])
        def _():
            source_y(a).wait_send()
            halo_y(a).wait_send()
        for b in range(2):
            @pl.when(jnp.logical_and(has_x[a], has_y[b]))
            def _():
                corner(a, b).wait_send()
    for store in stores:
        store.wait()


def local(curve_size, groups, field, source, mass, interp, parent_list, child_list, child_kind, counts):
    comps, rows_x, rows_y, nodes = field.shape
    slots = parent_list.shape[3]
    kinds = interp.shape[0]
    blocks = rows_x * rows_y
    deep = blocks + 2 * rows_y
    mem = comps * slots
    pieces = rows_x // 4 if rows_x % 4 == 0 else rows_x
    f32 = jnp.float32
    hbm = pl.BlockSpec(memory_space=pl.ANY)
    vmem = pl.BlockSpec(memory_space=pltpu.VMEM)
    smem = pl.BlockSpec(memory_space=pltpu.SMEM)
    dma = pltpu.SemaphoreType.DMA
    out = pl.pallas_call(
        functools.partial(kernel, curve_size, groups, rows_x, rows_y, nodes, slots, kinds, comps),
        out_shape=jax.ShapeDtypeStruct((comps, blocks, nodes), f32),
        in_specs=[hbm] * 4 + [smem] * 3 + [vmem] * 3,
        out_specs=hbm,
        scratch_shapes=[
            pltpu.VMEM((comps, deep, nodes), f32),
            pltpu.VMEM((comps, deep, nodes), f32),
            pltpu.VMEM((comps, blocks, nodes), f32),
            pltpu.VMEM((comps, deep, nodes), f32),
            pltpu.VMEM((deep, nodes), f32),
            pltpu.VMEM((comps, deep, nodes), f32),
            pltpu.VMEM((kinds * nodes, nodes), f32),
            pltpu.VMEM((groups, mem, nodes), f32),
            pltpu.VMEM((groups, mem, nodes), f32),
            pltpu.VMEM((groups * mem, nodes), f32),
            pltpu.VMEM((groups * mem, nodes), f32),
            pltpu.VMEM((groups, mem, nodes), f32),
            pltpu.VMEM((groups, mem, nodes), f32),
            pltpu.VMEM((2, comps, 2 * rows_y, nodes), f32),
            pltpu.VMEM((2, 2 * comps * rows_x, nodes), f32),
            pltpu.VMEM((2, 2 * comps * rows_x, nodes), f32),
            pltpu.VMEM((2, (comps + 1) * rows_x, nodes), f32),
            pltpu.VMEM((2, (comps + 1) * rows_x, nodes), f32),
            pltpu.VMEM((4, 8, nodes), f32),
            pltpu.VMEM((4, 8, nodes), f32),
            pltpu.VMEM((2, comps * rows_x, nodes), f32),
            pltpu.VMEM((deep, nodes), f32),
            dma((4,)),
            dma((pieces,)),
            dma((14,)),
            dma((14,)),
            dma((groups,)),
            dma((groups,)),
            dma((groups,)),
            dma((groups,)),
        ],
        compiler_params=pltpu.CompilerParams(
            collective_id=0, has_side_effects=True, vmem_limit_bytes=24 * 1024 * 1024
        ),
    )(
        field.reshape(comps, blocks, nodes),
        source.reshape(comps, blocks, nodes),
        mass.reshape(blocks, nodes),
        interp.reshape(kinds * nodes, nodes),
        parent_list, child_list, counts, parent_list, child_list, child_kind,
    )
    return out.reshape(comps, rows_x, rows_y, nodes)


def solution(mesh):
    in_specs = (
        P(None, "curve", "group", None),
        P(None, "curve", "group", None),
        P("curve", "group", None),
        P(),
        P("curve", "group", None, None),
        P("curve", "group", None, None),
        P("curve", "group", None, None),
        P("curve", "group", None),
    )
    out_specs = P(None, "curve", "group", None)
    body = functools.partial(local, mesh.shape["curve"], mesh.shape["group"])
    return jax.shard_map(body, mesh=mesh, in_specs=in_specs, out_specs=out_specs, check_vma=False)
```

```python
import functools

import jax
import jax.numpy as jnp
from jax import lax
from jax.experimental import pallas as pl
from jax.experimental.pallas import tpu as pltpu
from jax.sharding import PartitionSpec as P

OMEGA = 2.0 / 3.0
KEEP = 1.0 / 3.0
MESH = pl.DeviceIdType.MESH
NT = (((1,), (1,)), ((), ()))


def split(value):
    high = value.astype(jnp.bfloat16)
    low = (value - high.astype(jnp.float32)).astype(jnp.bfloat16)
    return high, low


def column(row, size):
    first = lax.broadcasted_iota(jnp.int32, (size, size), 0)
    second = lax.broadcasted_iota(jnp.int32, (size, size), 1)
    spread = jnp.where(first == second, jnp.broadcast_to(row.astype(jnp.float32), (size, size)), 0.0)
    return jnp.sum(spread, axis=1, keepdims=True)


def lane_row(columns, slots):
    groups = len(columns)
    width = 2 * groups * slots
    first = lax.broadcasted_iota(jnp.int32, (slots, width), 0)
    second = lax.broadcasted_iota(jnp.int32, (slots, width), 1)
    total = jnp.zeros((slots, width), jnp.float32)
    for half in range(2):
        for group, col in enumerate(columns):
            base = (half * groups + group) * slots
            total = total + jnp.where(second - base == first, jnp.broadcast_to(col, (slots, width)), 0.0)
    return jnp.sum(total, axis=0, keepdims=True).astype(jnp.int32)


def kernel(
    curve_size, groups, rows_x, rows_y, nodes, slots, kinds, comps,
    field, source, mass, interp, parent_list, child_list, child_kind, counts,
    fin,
    con, mid, src, wts, rhs, tab, pick, arr, base_rows, now_rows, res, back,
    x_in, y_out, y_in, s_out, s_in, k_out, k_in, y_mid, ext,
    parent_s, child_s, counts_s, parent_v, child_v, kind_v,
    load_sem, send_sem, recv_sem, pick_send, pick_recv, back_send, back_recv,
):
    f32 = jnp.float32
    blocks = rows_x * rows_y
    mem = comps * slots
    c = lax.axis_index("curve")
    g = lax.axis_index("group")
    has_x = (c > 0, c < curve_size - 1)
    has_y = (g > 0, g < groups - 1)
    step = (-1, 1)

    lists = [
        pltpu.make_async_copy(parent_list, parent_s, load_sem.at[4]),
        pltpu.make_async_copy(counts, counts_s, load_sem.at[5]),
        pltpu.make_async_copy(child_list, child_s, load_sem.at[6]),
        pltpu.make_async_copy(parent_list, parent_v, load_sem.at[7]),
        pltpu.make_async_copy(child_list, child_v, load_sem.at[8]),
        pltpu.make_async_copy(child_kind, kind_v, load_sem.at[9]),
    ]
    loads = [
        pltpu.make_async_copy(field, con.at[:, pl.ds(rows_y, blocks), :], load_sem.at[0]),
        pltpu.make_async_copy(mass, wts.at[pl.ds(rows_y, blocks), :], load_sem.at[1]),
        pltpu.make_async_copy(source, src.at[:, pl.ds(rows_y, blocks), :], load_sem.at[2]),
        pltpu.make_async_copy(interp, tab, load_sem.at[3]),
    ]
    loads[0].start()
    for load in lists + loads[1:]:
        load.start()

    barrier = pltpu.get_barrier_semaphore()
    for o in range(1, groups):
        pl.semaphore_signal(barrier, inc=1, device_id=(c, lax.rem(g + o, groups)), device_id_type=MESH)
    for a in range(2):
        @pl.when(has_x[a])
        def _():
            pl.semaphore_signal(barrier, inc=1, device_id=(c + step[a], g), device_id_type=MESH)
        for b in range(2):
            @pl.when(jnp.logical_and(has_x[a], has_y[b]))
            def _():
                pl.semaphore_signal(barrier, inc=1, device_id=(c + step[a], g + step[b]), device_id_type=MESH)
    one = lambda flag: jnp.where(flag, 1, 0)
    wide = one(has_x[0]) + one(has_x[1])
    tall = one(has_y[0]) + one(has_y[1])
    pl.semaphore_wait(barrier, groups - 1 + wide + wide * tall)

    def remote(src_ref, dst_ref, sent, landed, device):
        return pltpu.make_async_remote_copy(
            src_ref=src_ref, dst_ref=dst_ref, send_sem=send_sem.at[sent], recv_sem=recv_sem.at[landed],
            device_id=device, device_id_type=MESH,
        )

    def source_x(a, arriving=False):
        side = a if arriving else 1 - a
        edge = 0 if a == 0 else blocks - rows_y
        land = 0 if side == 0 else blocks + rows_y
        there = (c + step[a], g)
        return (
            remote(source.at[:, pl.ds(edge, rows_y), :], src.at[:, pl.ds(land, rows_y), :], a, side, there),
            remote(mass.at[pl.ds(edge, rows_y), :], wts.at[pl.ds(land, rows_y), :], 2 + a, 2 + side, there),
        )

    def source_y(b, arriving=False):
        side = b if arriving else 1 - b
        return remote(s_out.at[b], s_in.at[side], 4 + b, 4 + side, (c, g + step[b]))

    def halo_x(a, arriving=False):
        side = a if arriving else 1 - a
        edge = rows_y if a == 0 else blocks - rows_y
        return remote(con.at[:, pl.ds(edge, 2 * rows_y), :], x_in.at[side], 6 + a, 6 + side, (c + step[a], g))

    def halo_y(b, arriving=False):
        side = b if arriving else 1 - b
        return remote(y_out.at[b], y_in.at[side], 8 + b, 8 + side, (c, g + step[b]))

    def corner(a, b, arriving=False):
        side = 2 * a + b if arriving else 2 * (1 - a) + (1 - b)
        return remote(k_out.at[2 * a + b], k_in.at[side], 10 + 2 * a + b, 10 + side, (c + step[a], g + step[b]))

    def picks(o):
        d = lax.rem(g + o, groups)
        return pltpu.make_async_remote_copy(
            src_ref=pick.at[o], dst_ref=arr.at[g], send_sem=pick_send.at[o], recv_sem=pick_recv.at[o],
            device_id=(c, d), device_id_type=MESH,
        )

    def returns(o):
        d = lax.rem(g + o, groups)
        return pltpu.make_async_remote_copy(
            src_ref=res.at[d], dst_ref=back.at[g], send_sem=back_send.at[o], recv_sem=back_recv.at[o],
            device_id=(c, d), device_id_type=MESH,
        )

    for load in lists:
        load.wait()
    loads[0].wait()
    slot_of = lax.broadcasted_iota(jnp.int32, (slots, nodes), 0)
    for o in list(range(1, groups)) + [0]:
        d = lax.rem(g + o, groups)
        for k in range(slots):
            p = parent_s[0, 0, d, k]
            for m in range(comps):
                pick[o, pl.ds(m * slots + k, 1), :] = con[m, pl.ds(rows_y + p, 1), :]
        live = slot_of < counts_s[0, 0, d]
        for m in range(comps):
            part = pl.ds(m * slots, slots)
            pick[o, part, :] = jnp.where(live, pick[o, part, :], 0.0)
        if o:
            picks(o).start()
    arr[g] = pick[0]

    for a in range(2):
        @pl.when(has_x[a])
        def _():
            for copy in source_x(a):
                copy.start()

    loads[1].wait()
    loads[2].wait()
    for b in range(2):
        row = 0 if b == 0 else rows_y - 1
        for m in range(comps):
            s_out[b, pl.ds(m * rows_x, rows_x), :] = src[m, pl.ds(rows_y + row, rows_x, stride=rows_y), :]
        s_out[b, pl.ds(comps * rows_x, rows_x), :] = wts[pl.ds(rows_y + row, rows_x, stride=rows_y), :]

        @pl.when(has_y[b])
        def _():
            source_y(b).start()

    span = 2 * rows_y if rows_x % 2 == 0 else rows_y
    spans = blocks // span
    for t in range(spans):
        rows = pl.ds(rows_y + t * span, span)
        w = OMEGA / (6.0 + wts[rows, :])
        ext[pl.ds(rows_y + t * span, span), :] = w
        for m in range(comps):
            rhs[m, rows, :] = w * src[m, rows, :]
    zero_plane = jnp.zeros((rows_y, nodes), f32)
    for m in range(comps):
        con[m, pl.ds(0, rows_y), :] = zero_plane
        con[m, pl.ds(blocks + rows_y, rows_y), :] = zero_plane
    loads[3].wait()
    tab_high, tab_low = split(tab[...])
    kind_now = kind_v[0, 0]
    child_now = child_v[0, 0]
    parent_now = parent_v[0, 0]
    kind_of = []
    for s in range(groups):
        kind_col = jnp.broadcast_to(column(kind_now[s:s + 1, :], slots), (slots, nodes))
        kind_of += [kind_col] * comps
    kind_of = jnp.concatenate(kind_of, axis=0)
    child_row = lane_row([column(child_now[s:s + 1, :], slots) for s in range(groups)], slots)
    live_cols = []
    for s in range(groups):
        col = column(parent_now[s:s + 1, :], slots)
        ahead = lax.broadcasted_iota(jnp.int32, (slots, 1), 0) < counts_s[0, 0, s]
        live_cols.append(jnp.where(ahead, col, -1.0))
    parent_row = lane_row(live_cols, slots)

    def table_of(values):
        pieces = []
        for s in range(groups):
            pieces.append(jnp.concatenate(
                [values[(s * comps + m) * slots:(s * comps + m + 1) * slots, :] for m in range(comps)], axis=1))
        high, low = split(jnp.concatenate(pieces, axis=0))
        return jnp.concatenate([high, low], axis=0)

    piece = 4 * rows_y if rows_x % 4 == 0 else rows_y
    pieces = blocks // piece

    def spread(index_row, table, t):
        place = lax.broadcasted_iota(jnp.int32, (piece, 2 * groups * slots), 0) + t * piece
        hot = jnp.where(place == index_row, 1.0, 0.0).astype(jnp.bfloat16)
        return jnp.dot(hot, table, preferred_element_type=f32)

    for o in range(1, groups):
        picks(o).wait_recv()
    flat = arr[...].reshape(groups * mem, nodes)
    wide_rows = jnp.concatenate([jnp.where(kind_of == float(k), flat, 0.0) for k in range(kinds)], axis=1)
    high, low = split(wide_rows)
    hang = (
        jnp.dot(high, tab_high, preferred_element_type=f32)
        + jnp.dot(high, tab_low, preferred_element_type=f32)
        + jnp.dot(low, tab_high, preferred_element_type=f32)
    )
    table = table_of(hang)
    order = [0, pieces - 1] + list(range(1, pieces - 1))
    for at, t in enumerate(order):
        added = spread(child_row, table, t)
        for m in range(comps):
            rows = pl.ds(rows_y + t * piece, piece)
            con[m, rows, :] = con[m, rows, :] + added[:, m * nodes:(m + 1) * nodes]
        if at == 1:
            for a in range(2):
                @pl.when(has_x[a])
                def _():
                    halo_x(a).start()
            for a in range(2):
                for b in range(2):
                    x = 0 if a == 0 else rows_x - 1
                    y = 0 if b == 0 else rows_y - 1
                    for m in range(comps):
                        k_out[2 * a + b, pl.ds(m, 1), :] = con[m, pl.ds(rows_y + x * rows_y + y, 1), :]

                    @pl.when(jnp.logical_and(has_x[a], has_y[b]))
                    def _():
                        corner(a, b).start()
    for b in range(2):
        for j in range(2):
            row = j if b == 0 else rows_y - 1 - j
            for m in range(comps):
                y_out[b, pl.ds((j * comps + m) * rows_x, rows_x), :] = con[m, pl.ds(rows_y + row, rows_x, stride=rows_y), :]

        @pl.when(has_y[b])
        def _():
            halo_y(b).start()

    lane = lax.broadcasted_iota(jnp.int32, (1, nodes), 1)

    def along_z(v):
        up = jnp.where(lane == 0, 0.0, pltpu.roll(v, 1, 1))
        down = jnp.where(lane == nodes - 1, 0.0, pltpu.roll(v, nodes - 1, 1))
        return up + down

    sub = lax.broadcasted_iota(jnp.int32, (span, nodes), 0)
    is_first = sub == 0
    is_last = sub == rows_y - 1
    for t in range(1, span // rows_y):
        is_first = jnp.logical_or(is_first, sub == t * rows_y)
        is_last = jnp.logical_or(is_last, sub == (t + 1) * rows_y - 1)

    def core(state, m, t):
        at = rows_y + t * span
        centre = state[m, pl.ds(at, span), :]
        beside = state[m, pl.ds(at - rows_y, span), :] + state[m, pl.ds(at + rows_y, span), :]
        beside = beside + jnp.where(is_first, 0.0, state[m, pl.ds(at - 1, span), :])
        beside = beside + jnp.where(is_last, 0.0, state[m, pl.ds(at + 1, span), :])
        beside = beside + along_z(centre)
        return KEEP * centre + ext[pl.ds(at, span), :] * beside + rhs[m, pl.ds(at, span), :]

    for t in range(spans):
        for m in range(comps):
            mid[m, pl.ds(rows_y + t * span, span), :] = core(con, m, t)

    for s in range(groups):
        for k in range(slots):
            q = child_s[0, 0, s, k]
            for m in range(comps):
                base_rows[pl.ds((s * comps + m) * slots + k, 1), :] = con[m, pl.ds(rows_y + q, 1), :]

    for a in range(2):
        for b in range(2):
            both = jnp.logical_and(has_x[a], has_y[b])

            @pl.when(both)
            def _():
                corner(a, b, True).wait_recv()

            @pl.when(jnp.logical_not(both))
            def _():
                k_in[2 * a + b] = jnp.zeros((8, nodes), f32)
    top = lax.broadcasted_iota(jnp.int32, (rows_y, nodes), 0)
    for a in range(2):
        inside = rows_y if a == 0 else blocks
        plane = 0 if a == 0 else blocks + rows_y
        near = rows_y if a == 0 else 0
        far = 0 if a == 0 else rows_y

        @pl.when(has_x[a])
        def _():
            for copy in source_x(a, True):
                copy.wait_recv()
            halo_x(a, True).wait_recv()
            w_in = ext[pl.ds(inside, rows_y), :]
            w = OMEGA / (6.0 + wts[pl.ds(plane, rows_y), :])
            for m in range(comps):
                own = x_in[a, m, pl.ds(near, rows_y), :]
                mid[m, pl.ds(inside, rows_y), :] = mid[m, pl.ds(inside, rows_y), :] + w_in * own
                beside = x_in[a, m, pl.ds(far, rows_y), :] + con[m, pl.ds(inside, rows_y), :]
                low_end = jnp.broadcast_to(k_in[2 * a, pl.ds(m, 1), :], (rows_y, nodes))
                high_end = jnp.broadcast_to(k_in[2 * a + 1, pl.ds(m, 1), :], (rows_y, nodes))
                beside = beside + jnp.where(top == 0, low_end, pltpu.roll(own, 1, 0))
                beside = beside + jnp.where(top == rows_y - 1, high_end, pltpu.roll(own, rows_y - 1, 0))
                beside = beside + along_z(own) + src[m, pl.ds(plane, rows_y), :]
                mid[m, pl.ds(plane, rows_y), :] = KEEP * own + w * beside

        @pl.when(jnp.logical_not(has_x[a]))
        def _():
            for m in range(comps):
                mid[m, pl.ds(plane, rows_y), :] = zero_plane

    left = lax.broadcasted_iota(jnp.int32, (rows_x, nodes), 0)
    for b in range(2):
        row = 0 if b == 0 else rows_y - 1
        edge = pl.ds(rows_y + row, rows_x, stride=rows_y)

        @pl.when(has_y[b])
        def _():
            source_y(b, True).wait_recv()
            halo_y(b, True).wait_recv()
            w_in = ext[edge, :]
            w = OMEGA / (6.0 + s_in[b, pl.ds(comps * rows_x, rows_x), :])
            for m in range(comps):
                own = y_in[b, pl.ds(m * rows_x, rows_x), :]
                mid[m, edge, :] = mid[m, edge, :] + w_in * own
                beside = y_in[b, pl.ds((comps + m) * rows_x, rows_x), :] + con[m, edge, :]
                low_end = jnp.broadcast_to(k_in[b, pl.ds(m, 1), :], (rows_x, nodes))
                high_end = jnp.broadcast_to(k_in[2 + b, pl.ds(m, 1), :], (rows_x, nodes))
                beside = beside + jnp.where(left == 0, low_end, pltpu.roll(own, 1, 0))
                beside = beside + jnp.where(left == rows_x - 1, high_end, pltpu.roll(own, rows_x - 1, 0))
                beside = beside + along_z(own) + s_in[b, pl.ds(m * rows_x, rows_x), :]
                y_mid[b, pl.ds(m * rows_x, rows_x), :] = KEEP * own + w * beside

    for t in range(spans):
        for m in range(comps):
            fin[m, pl.ds(t * span, span), :] = core(mid, m, t)
    for b in range(2):
        row = 0 if b == 0 else rows_y - 1

        @pl.when(has_y[b])
        def _():
            w_in = ext[pl.ds(rows_y + row, rows_x, stride=rows_y), :]
            edge = pl.ds(row, rows_x, stride=rows_y)
            for m in range(comps):
                fin[m, edge, :] = fin[m, edge, :] + w_in * y_mid[b, pl.ds(m * rows_x, rows_x), :]

    for s in range(groups):
        for k in range(slots):
            q = child_s[0, 0, s, k]
            for m in range(comps):
                now_rows[pl.ds((s * comps + m) * slots + k, 1), :] = fin[m, pl.ds(q, 1), :]
    high, low = split(now_rows[...] - base_rows[...])
    product = (
        lax.dot_general(high, tab_high, NT, preferred_element_type=f32)
        + lax.dot_general(high, tab_low, NT, preferred_element_type=f32)
        + lax.dot_general(low, tab_high, NT, preferred_element_type=f32)
    )
    chosen = jnp.zeros((groups * mem, nodes), f32)
    for k in range(kinds):
        chosen = chosen + jnp.where(kind_of == float(k), product[:, k * nodes:(k + 1) * nodes], 0.0)
    res[...] = chosen.reshape(groups, mem, nodes)
    for o in range(1, groups):
        returns(o).start()
    back[g] = res[g]
    for o in range(1, groups):
        returns(o).wait_recv()
    table = table_of(back[...].reshape(groups * mem, nodes))
    for t in range(pieces):
        added = spread(parent_row, table, t)
        rows = pl.ds(t * piece, piece)
        for m in range(comps):
            fin[m, rows, :] = fin[m, rows, :] + added[:, m * nodes:(m + 1) * nodes]

    for o in range(1, groups):
        picks(o).wait_send()
        returns(o).wait_send()
    for a in range(2):
        @pl.when(has_x[a])
        def _():
            for copy in source_x(a):
                copy.wait_send()
            halo_x(a).wait_send()

        @pl.when(has_y[a])
        def _():
            source_y(a).wait_send()
            halo_y(a).wait_send()
        for b in range(2):
            @pl.when(jnp.logical_and(has_x[a], has_y[b]))
            def _():
                corner(a, b).wait_send()


def local(curve_size, groups, field, source, mass, interp, parent_list, child_list, child_kind, counts):
    comps, rows_x, rows_y, nodes = field.shape
    slots = parent_list.shape[3]
    kinds = interp.shape[0]
    blocks = rows_x * rows_y
    deep = blocks + 2 * rows_y
    mem = comps * slots
    f32 = jnp.float32
    hbm = pl.BlockSpec(memory_space=pltpu.HBM)
    vmem = pl.BlockSpec(memory_space=pltpu.VMEM)
    dma = pltpu.SemaphoreType.DMA
    out = pl.pallas_call(
        functools.partial(kernel, curve_size, groups, rows_x, rows_y, nodes, slots, kinds, comps),
        out_shape=jax.ShapeDtypeStruct((comps, blocks, nodes), f32),
        in_specs=[hbm] * 8,
        out_specs=vmem,
        scratch_shapes=[
            pltpu.VMEM((comps, deep, nodes), f32),
            pltpu.VMEM((comps, deep, nodes), f32),
            pltpu.VMEM((comps, deep, nodes), f32),
            pltpu.VMEM((deep, nodes), f32),
            pltpu.VMEM((comps, deep, nodes), f32),
            pltpu.VMEM((kinds * nodes, nodes), f32),
            pltpu.VMEM((groups, mem, nodes), f32),
            pltpu.VMEM((groups, mem, nodes), f32),
            pltpu.VMEM((groups * mem, nodes), f32),
            pltpu.VMEM((groups * mem, nodes), f32),
            pltpu.VMEM((groups, mem, nodes), f32),
            pltpu.VMEM((groups, mem, nodes), f32),
            pltpu.VMEM((2, comps, 2 * rows_y, nodes), f32),
            pltpu.VMEM((2, 2 * comps * rows_x, nodes), f32),
            pltpu.VMEM((2, 2 * comps * rows_x, nodes), f32),
            pltpu.VMEM((2, (comps + 1) * rows_x, nodes), f32),
            pltpu.VMEM((2, (comps + 1) * rows_x, nodes), f32),
            pltpu.VMEM((4, 8, nodes), f32),
            pltpu.VMEM((4, 8, nodes), f32),
            pltpu.VMEM((2, comps * rows_x, nodes), f32),
            pltpu.VMEM((deep, nodes), f32),
            pltpu.SMEM(parent_list.shape, jnp.int32),
            pltpu.SMEM(child_list.shape, jnp.int32),
            pltpu.SMEM(counts.shape, jnp.int32),
            pltpu.VMEM(parent_list.shape, jnp.int32),
            pltpu.VMEM(child_list.shape, jnp.int32),
            pltpu.VMEM(child_kind.shape, jnp.int32),
            dma((10,)),
            dma((14,)),
            dma((14,)),
            dma((groups,)),
            dma((groups,)),
            dma((groups,)),
            dma((groups,)),
        ],
        compiler_params=pltpu.CompilerParams(
            collective_id=0, has_side_effects=True, vmem_limit_bytes=60 * 1024 * 1024
        ),
    )(
        field.reshape(comps, blocks, nodes),
        source.reshape(comps, blocks, nodes),
        mass.reshape(blocks, nodes),
        interp.reshape(kinds * nodes, nodes),
        parent_list, child_list, child_kind, counts,
    )
    return out.reshape(comps, rows_x, rows_y, nodes)


def solution(mesh):
    in_specs = (
        P(None, "curve", "group", None),
        P(None, "curve", "group", None),
        P("curve", "group", None),
        P(),
        P("curve", "group", None, None),
        P("curve", "group", None, None),
        P("curve", "group", None, None),
        P("curve", "group", None),
    )
    out_specs = P(None, "curve", "group", None)
    body = functools.partial(local, mesh.shape["curve"], mesh.shape["group"])
    return jax.shard_map(body, mesh=mesh, in_specs=in_specs, out_specs=out_specs, check_vma=False)
```

```python
import functools

import jax
import jax.numpy as jnp
from jax import lax
from jax.experimental import pallas as pl
from jax.experimental.pallas import tpu as pltpu
from jax.sharding import PartitionSpec as P

OMEGA = 2.0 / 3.0
KEEP = 1.0 / 3.0
MESH = pl.DeviceIdType.MESH
NT = (((1,), (1,)), ((), ()))


def split(value):
    high = value.astype(jnp.bfloat16)
    low = (value - high.astype(jnp.float32)).astype(jnp.bfloat16)
    return high, low


def column(row, size):
    first = lax.broadcasted_iota(jnp.int32, (size, size), 0)
    second = lax.broadcasted_iota(jnp.int32, (size, size), 1)
    spread = jnp.where(first == second, jnp.broadcast_to(row.astype(jnp.float32), (size, size)), 0.0)
    return jnp.sum(spread, axis=1, keepdims=True)


def lane_row(columns, slots):
    groups = len(columns)
    width = 2 * groups * slots
    first = lax.broadcasted_iota(jnp.int32, (slots, width), 0)
    second = lax.broadcasted_iota(jnp.int32, (slots, width), 1)
    total = jnp.zeros((slots, width), jnp.float32)
    for half in range(2):
        for group, col in enumerate(columns):
            base = (half * groups + group) * slots
            total = total + jnp.where(second - base == first, jnp.broadcast_to(col, (slots, width)), 0.0)
    return jnp.sum(total, axis=0, keepdims=True).astype(jnp.int32)


def kernel(
    curve_size, groups, rows_x, rows_y, nodes, slots, kinds, comps,
    field, source, mass, interp, parent_list, child_list, child_kind, counts,
    out,
    con, mid, fin, src, wts, rhs, tab, pick, arr, base_rows, now_rows, res, back,
    x_in, y_out, y_in, s_out, s_in, k_out, k_in, y_mid, ext,
    parent_s, child_s, counts_s, parent_v, child_v, kind_v,
    load_sem, out_sem, send_sem, recv_sem, pick_send, pick_recv, back_send, back_recv,
):
    f32 = jnp.float32
    blocks = rows_x * rows_y
    mem = comps * slots
    c = lax.axis_index("curve")
    g = lax.axis_index("group")
    has_x = (c > 0, c < curve_size - 1)
    has_y = (g > 0, g < groups - 1)
    step = (-1, 1)

    lists = [
        pltpu.make_async_copy(parent_list, parent_s, load_sem.at[4]),
        pltpu.make_async_copy(counts, counts_s, load_sem.at[5]),
        pltpu.make_async_copy(child_list, child_s, load_sem.at[6]),
        pltpu.make_async_copy(parent_list, parent_v, load_sem.at[7]),
        pltpu.make_async_copy(child_list, child_v, load_sem.at[8]),
        pltpu.make_async_copy(child_kind, kind_v, load_sem.at[9]),
    ]
    loads = [
        pltpu.make_async_copy(field, con.at[:, pl.ds(rows_y, blocks), :], load_sem.at[0]),
        pltpu.make_async_copy(mass, wts.at[pl.ds(rows_y, blocks), :], load_sem.at[1]),
        pltpu.make_async_copy(source, src.at[:, pl.ds(rows_y, blocks), :], load_sem.at[2]),
        pltpu.make_async_copy(interp, tab, load_sem.at[3]),
    ]
    loads[0].start()
    for load in lists + loads[1:]:
        load.start()

    barrier = pltpu.get_barrier_semaphore()
    for o in range(1, groups):
        pl.semaphore_signal(barrier, inc=1, device_id=(c, lax.rem(g + o, groups)), device_id_type=MESH)
    for a in range(2):
        @pl.when(has_x[a])
        def _():
            pl.semaphore_signal(barrier, inc=1, device_id=(c + step[a], g), device_id_type=MESH)
        for b in range(2):
            @pl.when(jnp.logical_and(has_x[a], has_y[b]))
            def _():
                pl.semaphore_signal(barrier, inc=1, device_id=(c + step[a], g + step[b]), device_id_type=MESH)
    one = lambda flag: jnp.where(flag, 1, 0)
    wide = one(has_x[0]) + one(has_x[1])
    tall = one(has_y[0]) + one(has_y[1])
    pl.semaphore_wait(barrier, groups - 1 + wide + wide * tall)

    def remote(src_ref, dst_ref, sent, landed, device):
        return pltpu.make_async_remote_copy(
            src_ref=src_ref, dst_ref=dst_ref, send_sem=send_sem.at[sent], recv_sem=recv_sem.at[landed],
            device_id=device, device_id_type=MESH,
        )

    def source_x(a, arriving=False):
        side = a if arriving else 1 - a
        edge = 0 if a == 0 else blocks - rows_y
        land = 0 if side == 0 else blocks + rows_y
        there = (c + step[a], g)
        return (
            remote(source.at[:, pl.ds(edge, rows_y), :], src.at[:, pl.ds(land, rows_y), :], a, side, there),
            remote(mass.at[pl.ds(edge, rows_y), :], wts.at[pl.ds(land, rows_y), :], 2 + a, 2 + side, there),
        )

    def source_y(b, arriving=False):
        side = b if arriving else 1 - b
        return remote(s_out.at[b], s_in.at[side], 4 + b, 4 + side, (c, g + step[b]))

    def halo_x(a, arriving=False):
        side = a if arriving else 1 - a
        edge = rows_y if a == 0 else blocks - rows_y
        return remote(con.at[:, pl.ds(edge, 2 * rows_y), :], x_in.at[side], 6 + a, 6 + side, (c + step[a], g))

    def halo_y(b, arriving=False):
        side = b if arriving else 1 - b
        return remote(y_out.at[b], y_in.at[side], 8 + b, 8 + side, (c, g + step[b]))

    def corner(a, b, arriving=False):
        side = 2 * a + b if arriving else 2 * (1 - a) + (1 - b)
        return remote(k_out.at[2 * a + b], k_in.at[side], 10 + 2 * a + b, 10 + side, (c + step[a], g + step[b]))

    def picks(o):
        d = lax.rem(g + o, groups)
        return pltpu.make_async_remote_copy(
            src_ref=pick.at[o], dst_ref=arr.at[g], send_sem=pick_send.at[o], recv_sem=pick_recv.at[o],
            device_id=(c, d), device_id_type=MESH,
        )

    def returns(o):
        d = lax.rem(g + o, groups)
        return pltpu.make_async_remote_copy(
            src_ref=res.at[d], dst_ref=back.at[g], send_sem=back_send.at[o], recv_sem=back_recv.at[o],
            device_id=(c, d), device_id_type=MESH,
        )

    for load in lists:
        load.wait()
    loads[0].wait()
    slot_of = lax.broadcasted_iota(jnp.int32, (slots, nodes), 0)
    for o in list(range(1, groups)) + [0]:
        d = lax.rem(g + o, groups)
        for k in range(slots):
            p = parent_s[0, 0, d, k]
            for m in range(comps):
                pick[o, pl.ds(m * slots + k, 1), :] = con[m, pl.ds(rows_y + p, 1), :]
        live = slot_of < counts_s[0, 0, d]
        for m in range(comps):
            part = pl.ds(m * slots, slots)
            pick[o, part, :] = jnp.where(live, pick[o, part, :], 0.0)
        if o:
            picks(o).start()
    arr[g] = pick[0]

    for a in range(2):
        @pl.when(has_x[a])
        def _():
            for copy in source_x(a):
                copy.start()

    loads[1].wait()
    loads[2].wait()
    for b in range(2):
        row = 0 if b == 0 else rows_y - 1
        for m in range(comps):
            s_out[b, pl.ds(m * rows_x, rows_x), :] = src[m, pl.ds(rows_y + row, rows_x, stride=rows_y), :]
        s_out[b, pl.ds(comps * rows_x, rows_x), :] = wts[pl.ds(rows_y + row, rows_x, stride=rows_y), :]

        @pl.when(has_y[b])
        def _():
            source_y(b).start()

    span = 2 * rows_y if rows_x % 2 == 0 else rows_y
    spans = blocks // span
    for t in range(spans):
        rows = pl.ds(rows_y + t * span, span)
        w = OMEGA / (6.0 + wts[rows, :])
        ext[pl.ds(rows_y + t * span, span), :] = w
        for m in range(comps):
            rhs[m, rows, :] = w * src[m, rows, :]
    zero_plane = jnp.zeros((rows_y, nodes), f32)
    for m in range(comps):
        con[m, pl.ds(0, rows_y), :] = zero_plane
        con[m, pl.ds(blocks + rows_y, rows_y), :] = zero_plane
    loads[3].wait()
    tab_high, tab_low = split(tab[...])
    kind_now = kind_v[0, 0]
    child_now = child_v[0, 0]
    parent_now = parent_v[0, 0]
    kind_of = []
    for s in range(groups):
        kind_col = jnp.broadcast_to(column(kind_now[s:s + 1, :], slots), (slots, nodes))
        kind_of += [kind_col] * comps
    kind_of = jnp.concatenate(kind_of, axis=0)
    child_row = lane_row([column(child_now[s:s + 1, :], slots) for s in range(groups)], slots)
    live_cols = []
    for s in range(groups):
        col = column(parent_now[s:s + 1, :], slots)
        ahead = lax.broadcasted_iota(jnp.int32, (slots, 1), 0) < counts_s[0, 0, s]
        live_cols.append(jnp.where(ahead, col, -1.0))
    parent_row = lane_row(live_cols, slots)

    def table_of(values):
        pieces = []
        for s in range(groups):
            pieces.append(jnp.concatenate(
                [values[(s * comps + m) * slots:(s * comps + m + 1) * slots, :] for m in range(comps)], axis=1))
        high, low = split(jnp.concatenate(pieces, axis=0))
        return jnp.concatenate([high, low], axis=0)

    piece = 4 * rows_y if rows_x % 4 == 0 else rows_y
    pieces = blocks // piece

    def spread(index_row, table, t):
        place = lax.broadcasted_iota(jnp.int32, (piece, 2 * groups * slots), 0) + t * piece
        hot = jnp.where(place == index_row, 1.0, 0.0).astype(jnp.bfloat16)
        return jnp.dot(hot, table, preferred_element_type=f32)

    for o in range(1, groups):
        picks(o).wait_recv()
    flat = arr[...].reshape(groups * mem, nodes)
    wide_rows = jnp.concatenate([jnp.where(kind_of == float(k), flat, 0.0) for k in range(kinds)], axis=1)
    high, low = split(wide_rows)
    hang = (
        jnp.dot(high, tab_high, preferred_element_type=f32)
        + jnp.dot(high, tab_low, preferred_element_type=f32)
        + jnp.dot(low, tab_high, preferred_element_type=f32)
    )
    table = table_of(hang)
    order = [0, pieces - 1] + list(range(1, pieces - 1))
    for at, t in enumerate(order):
        added = spread(child_row, table, t)
        for m in range(comps):
            rows = pl.ds(rows_y + t * piece, piece)
            con[m, rows, :] = con[m, rows, :] + added[:, m * nodes:(m + 1) * nodes]
        if at == 1:
            for a in range(2):
                @pl.when(has_x[a])
                def _():
                    halo_x(a).start()
            for a in range(2):
                for b in range(2):
                    x = 0 if a == 0 else rows_x - 1
                    y = 0 if b == 0 else rows_y - 1
                    for m in range(comps):
                        k_out[2 * a + b, pl.ds(m, 1), :] = con[m, pl.ds(rows_y + x * rows_y + y, 1), :]

                    @pl.when(jnp.logical_and(has_x[a], has_y[b]))
                    def _():
                        corner(a, b).start()
    for b in range(2):
        for j in range(2):
            row = j if b == 0 else rows_y - 1 - j
            for m in range(comps):
                y_out[b, pl.ds((j * comps + m) * rows_x, rows_x), :] = con[m, pl.ds(rows_y + row, rows_x, stride=rows_y), :]

        @pl.when(has_y[b])
        def _():
            halo_y(b).start()

    lane = lax.broadcasted_iota(jnp.int32, (1, nodes), 1)

    def along_z(v):
        up = jnp.where(lane == 0, 0.0, pltpu.roll(v, 1, 1))
        down = jnp.where(lane == nodes - 1, 0.0, pltpu.roll(v, nodes - 1, 1))
        return up + down

    sub = lax.broadcasted_iota(jnp.int32, (span, nodes), 0)
    is_first = sub == 0
    is_last = sub == rows_y - 1
    for t in range(1, span // rows_y):
        is_first = jnp.logical_or(is_first, sub == t * rows_y)
        is_last = jnp.logical_or(is_last, sub == (t + 1) * rows_y - 1)

    def core(state, m, t):
        at = rows_y + t * span
        centre = state[m, pl.ds(at, span), :]
        beside = state[m, pl.ds(at - rows_y, span), :] + state[m, pl.ds(at + rows_y, span), :]
        beside = beside + jnp.where(is_first, 0.0, state[m, pl.ds(at - 1, span), :])
        beside = beside + jnp.where(is_last, 0.0, state[m, pl.ds(at + 1, span), :])
        beside = beside + along_z(centre)
        return KEEP * centre + ext[pl.ds(at, span), :] * beside + rhs[m, pl.ds(at, span), :]

    for t in range(spans):
        for m in range(comps):
            mid[m, pl.ds(rows_y + t * span, span), :] = core(con, m, t)

    for s in range(groups):
        for k in range(slots):
            q = child_s[0, 0, s, k]
            for m in range(comps):
                base_rows[pl.ds((s * comps + m) * slots + k, 1), :] = con[m, pl.ds(rows_y + q, 1), :]

    for a in range(2):
        for b in range(2):
            both = jnp.logical_and(has_x[a], has_y[b])

            @pl.when(both)
            def _():
                corner(a, b, True).wait_recv()

            @pl.when(jnp.logical_not(both))
            def _():
                k_in[2 * a + b] = jnp.zeros((8, nodes), f32)
    top = lax.broadcasted_iota(jnp.int32, (rows_y, nodes), 0)
    for a in range(2):
        inside = rows_y if a == 0 else blocks
        plane = 0 if a == 0 else blocks + rows_y
        near = rows_y if a == 0 else 0
        far = 0 if a == 0 else rows_y

        @pl.when(has_x[a])
        def _():
            for copy in source_x(a, True):
                copy.wait_recv()
            halo_x(a, True).wait_recv()
            w_in = ext[pl.ds(inside, rows_y), :]
            w = OMEGA / (6.0 + wts[pl.ds(plane, rows_y), :])
            for m in range(comps):
                own = x_in[a, m, pl.ds(near, rows_y), :]
                mid[m, pl.ds(inside, rows_y), :] = mid[m, pl.ds(inside, rows_y), :] + w_in * own
                beside = x_in[a, m, pl.ds(far, rows_y), :] + con[m, pl.ds(inside, rows_y), :]
                low_end = jnp.broadcast_to(k_in[2 * a, pl.ds(m, 1), :], (rows_y, nodes))
                high_end = jnp.broadcast_to(k_in[2 * a + 1, pl.ds(m, 1), :], (rows_y, nodes))
                beside = beside + jnp.where(top == 0, low_end, pltpu.roll(own, 1, 0))
                beside = beside + jnp.where(top == rows_y - 1, high_end, pltpu.roll(own, rows_y - 1, 0))
                beside = beside + along_z(own) + src[m, pl.ds(plane, rows_y), :]
                mid[m, pl.ds(plane, rows_y), :] = KEEP * own + w * beside

        @pl.when(jnp.logical_not(has_x[a]))
        def _():
            for m in range(comps):
                mid[m, pl.ds(plane, rows_y), :] = zero_plane

    left = lax.broadcasted_iota(jnp.int32, (rows_x, nodes), 0)
    for b in range(2):
        row = 0 if b == 0 else rows_y - 1
        edge = pl.ds(rows_y + row, rows_x, stride=rows_y)

        @pl.when(has_y[b])
        def _():
            source_y(b, True).wait_recv()
            halo_y(b, True).wait_recv()
            w_in = ext[edge, :]
            w = OMEGA / (6.0 + s_in[b, pl.ds(comps * rows_x, rows_x), :])
            for m in range(comps):
                own = y_in[b, pl.ds(m * rows_x, rows_x), :]
                mid[m, edge, :] = mid[m, edge, :] + w_in * own
                beside = y_in[b, pl.ds((comps + m) * rows_x, rows_x), :] + con[m, edge, :]
                low_end = jnp.broadcast_to(k_in[b, pl.ds(m, 1), :], (rows_x, nodes))
                high_end = jnp.broadcast_to(k_in[2 + b, pl.ds(m, 1), :], (rows_x, nodes))
                beside = beside + jnp.where(left == 0, low_end, pltpu.roll(own, 1, 0))
                beside = beside + jnp.where(left == rows_x - 1, high_end, pltpu.roll(own, rows_x - 1, 0))
                beside = beside + along_z(own) + s_in[b, pl.ds(m * rows_x, rows_x), :]
                y_mid[b, pl.ds(m * rows_x, rows_x), :] = KEEP * own + w * beside

    for t in range(spans):
        for m in range(comps):
            fin[m, pl.ds(t * span, span), :] = core(mid, m, t)
    for b in range(2):
        row = 0 if b == 0 else rows_y - 1

        @pl.when(has_y[b])
        def _():
            w_in = ext[pl.ds(rows_y + row, rows_x, stride=rows_y), :]
            edge = pl.ds(row, rows_x, stride=rows_y)
            for m in range(comps):
                fin[m, edge, :] = fin[m, edge, :] + w_in * y_mid[b, pl.ds(m * rows_x, rows_x), :]

    for s in range(groups):
        for k in range(slots):
            q = child_s[0, 0, s, k]
            for m in range(comps):
                now_rows[pl.ds((s * comps + m) * slots + k, 1), :] = fin[m, pl.ds(q, 1), :]
    high, low = split(now_rows[...] - base_rows[...])
    product = (
        lax.dot_general(high, tab_high, NT, preferred_element_type=f32)
        + lax.dot_general(high, tab_low, NT, preferred_element_type=f32)
        + lax.dot_general(low, tab_high, NT, preferred_element_type=f32)
    )
    chosen = jnp.zeros((groups * mem, nodes), f32)
    for k in range(kinds):
        chosen = chosen + jnp.where(kind_of == float(k), product[:, k * nodes:(k + 1) * nodes], 0.0)
    res[...] = chosen.reshape(groups, mem, nodes)
    for o in range(1, groups):
        returns(o).start()
    back[g] = res[g]
    for o in range(1, groups):
        returns(o).wait_recv()
    table = table_of(back[...].reshape(groups * mem, nodes))
    stores = []
    for t in range(pieces):
        added = spread(parent_row, table, t)
        rows = pl.ds(t * piece, piece)
        for m in range(comps):
            fin[m, rows, :] = fin[m, rows, :] + added[:, m * nodes:(m + 1) * nodes]
        store = pltpu.make_async_copy(fin.at[:, rows, :], out.at[:, rows, :], out_sem.at[t])
        store.start()
        stores.append(store)

    for o in range(1, groups):
        picks(o).wait_send()
        returns(o).wait_send()
    for a in range(2):
        @pl.when(has_x[a])
        def _():
            for copy in source_x(a):
                copy.wait_send()
            halo_x(a).wait_send()

        @pl.when(has_y[a])
        def _():
            source_y(a).wait_send()
            halo_y(a).wait_send()
        for b in range(2):
            @pl.when(jnp.logical_and(has_x[a], has_y[b]))
            def _():
                corner(a, b).wait_send()
    for store in stores:
        store.wait()


def local(curve_size, groups, field, source, mass, interp, parent_list, child_list, child_kind, counts):
    comps, rows_x, rows_y, nodes = field.shape
    slots = parent_list.shape[3]
    kinds = interp.shape[0]
    blocks = rows_x * rows_y
    deep = blocks + 2 * rows_y
    mem = comps * slots
    f32 = jnp.float32
    hbm = pl.BlockSpec(memory_space=pltpu.HBM)
    dma = pltpu.SemaphoreType.DMA
    out = pl.pallas_call(
        functools.partial(kernel, curve_size, groups, rows_x, rows_y, nodes, slots, kinds, comps),
        out_shape=jax.ShapeDtypeStruct((comps, blocks, nodes), f32),
        in_specs=[hbm] * 8,
        out_specs=hbm,
        scratch_shapes=[
            pltpu.VMEM((comps, deep, nodes), f32),
            pltpu.VMEM((comps, deep, nodes), f32),
            pltpu.VMEM((comps, blocks, nodes), f32),
            pltpu.VMEM((comps, deep, nodes), f32),
            pltpu.VMEM((deep, nodes), f32),
            pltpu.VMEM((comps, deep, nodes), f32),
            pltpu.VMEM((kinds * nodes, nodes), f32),
            pltpu.VMEM((groups, mem, nodes), f32),
            pltpu.VMEM((groups, mem, nodes), f32),
            pltpu.VMEM((groups * mem, nodes), f32),
            pltpu.VMEM((groups * mem, nodes), f32),
            pltpu.VMEM((groups, mem, nodes), f32),
            pltpu.VMEM((groups, mem, nodes), f32),
            pltpu.VMEM((2, comps, 2 * rows_y, nodes), f32),
            pltpu.VMEM((2, 2 * comps * rows_x, nodes), f32),
            pltpu.VMEM((2, 2 * comps * rows_x, nodes), f32),
            pltpu.VMEM((2, (comps + 1) * rows_x, nodes), f32),
            pltpu.VMEM((2, (comps + 1) * rows_x, nodes), f32),
            pltpu.VMEM((4, 8, nodes), f32),
            pltpu.VMEM((4, 8, nodes), f32),
            pltpu.VMEM((2, comps * rows_x, nodes), f32),
            pltpu.VMEM((deep, nodes), f32),
            pltpu.SMEM(parent_list.shape, jnp.int32),
            pltpu.SMEM(child_list.shape, jnp.int32),
            pltpu.SMEM(counts.shape, jnp.int32),
            pltpu.VMEM(parent_list.shape, jnp.int32),
            pltpu.VMEM(child_list.shape, jnp.int32),
            pltpu.VMEM(child_kind.shape, jnp.int32),
            dma((10,)),
            dma((rows_x // 4 if rows_x % 4 == 0 else rows_x,)),
            dma((14,)),
            dma((14,)),
            dma((groups,)),
            dma((groups,)),
            dma((groups,)),
            dma((groups,)),
        ],
        compiler_params=pltpu.CompilerParams(
            collective_id=0, has_side_effects=True, vmem_limit_bytes=60 * 1024 * 1024
        ),
    )(
        field.reshape(comps, blocks, nodes),
        source.reshape(comps, blocks, nodes),
        mass.reshape(blocks, nodes),
        interp.reshape(kinds * nodes, nodes),
        parent_list, child_list, child_kind, counts,
    )
    return out.reshape(comps, rows_x, rows_y, nodes)


def solution(mesh):
    in_specs = (
        P(None, "curve", "group", None),
        P(None, "curve", "group", None),
        P("curve", "group", None),
        P(),
        P("curve", "group", None, None),
        P("curve", "group", None, None),
        P("curve", "group", None, None),
        P("curve", "group", None),
    )
    out_specs = P(None, "curve", "group", None)
    body = functools.partial(local, mesh.shape["curve"], mesh.shape["group"])
    return jax.shard_map(body, mesh=mesh, in_specs=in_specs, out_specs=out_specs, check_vma=False)
```
